32 devices in a mesh: ctx: 8 (over z, y), head: 4 (over x, core).
Axes of the slice: x: 2, y: 2, z: 4, core: 2. Of those that a mesh axis runs over, the one named last changes fastest.
Arguments:
- linear_query: bfloat16 [2048, 8192], P('ctx', 'head'), may hold values from -6 to 6
- linear_key: bfloat16 [2048, 8192], P('ctx', 'head'), may hold values from -6 to 6
- linear_value: bfloat16 [2048, 8192], P('ctx', 'head'), may hold values from -6 to 6
- log_decay: float32 [64, 2048], P('head', 'ctx'), may hold values from -1.2 to 0, as said below
- norm_gain: float32 [8192], P('head'), may hold values from 0.25 to 1.75
- soft_query: bfloat16 [2048, 8192], P('ctx', 'head'), may hold values from -4.5 to 4.5
- soft_key: bfloat16 [2048, 8192], P('ctx', 'head'), may hold values from -4.5 to 4.5
- soft_value: bfloat16 [2048, 8192], P('ctx', 'head'), may hold values from -6 to 6
- block_index: int32 [16, 5], P('ctx'), may hold values from 0 to 15, as said below
- block_count: int32 [16], P('ctx'), may hold values from 1 to 5, as said below
Outputs:
- linear_rows: bfloat16 [2048, 8192], P(('ctx', 'head'))
- softmax_rows: bfloat16 [2048, 8192], P(('ctx', 'head'))
The draws below stay inside these ranges and needn't reach their ends.
Inputs may be any that keep to these rules, and one draw needn't show every extreme that they name: `block_index`: entry 0 of row r is r itself; entries 1 to block_count[r] - 1 are distinct blocks from r - 4 to r - 1, and the farthest of them, r - 4, is named in some row; the entries from block_count[r] on equal r. `block_count`: at most r + 1 for row r; 5 in some row. `log_decay`: strictly negative.
All inputs are finite; a program needn't handle non-finite values.
Results may differ from the reference program's by a relative error of at most 0.0057.
Values may be sent and summed in bfloat16 or wider, within the bound.
A program may use at most 192 MiB of HBM per device.

```python
import math
import jax
import jax.numpy as jnp
from jax import lax

H = 64
HD = 128
SEC = 256
BLK = 128
KMAX = 5
WIN_SEC = 2
CONTEXT_TOKENS = 2048
QBLOCKS = 16


def draw_log_decay(key, part):
    every_key = jax.random.split(key, 7)
    fast_share = 50
    heads_fast = jax.random.randint(every_key[0], (H,), 0, 100) < fast_share
    fast_rate = jnp.exp(jax.random.uniform(every_key[1], (H,), minval=math.log(1.0 / 50.0), maxval=math.log(1.0 / 25.0)))
    slow_rate = jnp.exp(jax.random.uniform(every_key[2], (H,), minval=0.0, maxval=math.log(2.0))) * (0.2 / CONTEXT_TOKENS)
    baseline_rate = jnp.where(heads_fast, fast_rate, slow_rate)
    sections = CONTEXT_TOKENS // SEC
    section_factor = jnp.exp(jax.random.uniform(every_key[3], (H, sections), minval=math.log(0.5), maxval=math.log(2.0)))
    quiet_sections = jax.random.bernoulli(jax.random.fold_in(key, 9), 0.5, (H, sections))
    section_factor = jnp.where(heads_fast[:, None] & quiet_sections, section_factor * 0.005, section_factor)
    token_multiplier = jnp.repeat(section_factor, SEC, axis=1)
    jaggedness = jax.random.uniform(every_key[4], (H, CONTEXT_TOKENS), minval=0.5, maxval=1.5)
    spike_locations = jax.random.randint(every_key[5], (2,), 0, CONTEXT_TOKENS)
    spike_depth = jnp.log(jax.random.uniform(every_key[6], (2,), minval=0.6, maxval=0.8))
    token_positions = jnp.arange(CONTEXT_TOKENS, dtype=jnp.int32)
    spike_events = jnp.sum(jnp.where(token_positions[None, :] == spike_locations[:, None], spike_depth[:, None], 0.0), axis=0)
    return (-baseline_rate[:, None] * token_multiplier * jaggedness + spike_events[None, :]).astype(jnp.float32)


def drawn_field(key):
    return jax.random.truncated_normal(key, -4.5, 4.5, (CONTEXT_TOKENS, H * HD))


def draw_soft_key(key, part):
    values_drawn = drawn_field(jax.random.fold_in(key, 1)).reshape(QBLOCKS, BLK, H, HD)
    return values_drawn.reshape(CONTEXT_TOKENS, H * HD).astype(jnp.bfloat16)


def draw_soft_query(key, part):
    values_drawn = drawn_field(jax.random.fold_in(key, 2)).reshape(QBLOCKS, BLK, H, HD)
    return values_drawn.reshape(CONTEXT_TOKENS, H * HD).astype(jnp.bfloat16)


def pattern_tables(key):
    base = jax.random.fold_in(key, 11)
    key_floor, key_count, key_order = jax.random.split(base, 3)
    per_section = SEC // BLK
    span = WIN_SEC * per_section
    rows_all = jnp.arange(QBLOCKS, dtype=jnp.int32)
    floors = jnp.repeat(jax.random.randint(key_floor, (QBLOCKS // per_section,), 1, KMAX + 1), per_section)
    counts = jax.random.randint(key_count, (QBLOCKS,), floors, KMAX + 1)
    counts = jnp.minimum(counts, rows_all + 1)
    is_last = rows_all == QBLOCKS - 1
    counts = jnp.where(is_last, KMAX, counts)
    orders = jax.vmap(lambda subkey: jax.random.permutation(subkey, span))(jax.random.split(key_order, QBLOCKS))
    offsets = jnp.arange(1, span + 1, dtype=jnp.int32)
    beyond = (offsets[None, :] > rows_all[:, None]).astype(jnp.int32)
    farthest = (is_last[:, None] & (offsets[None, :] == span)).astype(jnp.int32)
    scores = orders.astype(jnp.int32) + span * beyond - 2 * span * farthest
    chosen = jnp.argsort(scores, axis=1, stable=True)[:, :KMAX - 1].astype(jnp.int32) + 1
    others = rows_all[:, None] - chosen
    slots = jnp.arange(1, KMAX, dtype=jnp.int32)
    others = jnp.where(slots[None, :] < counts[:, None], others, rows_all[:, None])
    index = jnp.concatenate([rows_all[:, None], others], axis=1)
    return (index.astype(jnp.int32), counts.astype(jnp.int32))


def draw_block_index(key, part):
    return pattern_tables(key)[0]


def draw_block_count(key, part):
    return pattern_tables(key)[1]


def block_scale(rng, dims, cuts, smallest, high):
    level, own = 1.0, jax.random.fold_in(rng, 6)
    for dim, blocks in cuts:
        steps = jnp.exp(jax.random.uniform(jax.random.fold_in(own, dim), (blocks,), jnp.float32, smallest / len(cuts), high / len(cuts)))
        level = level * jnp.repeat(steps, dims[dim] // blocks).reshape([-1 if axis == dim else 1 for axis in range(len(dims))])
    return level


def centred(own_key, extent, deviation, most, cuts=(), held_as=jnp.bfloat16):
    result = jax.random.normal(own_key, extent, jnp.float32) * deviation
    if len(cuts) > 0:
        result = block_scale(own_key, extent, cuts, -0.22, 0.18) * result
    return jnp.clip(result, min=-most, max=most).astype(held_as)


def setup_inputs(seed: int = 0) -> dict:
    key_list = jax.random.split(jax.random.key(seed), 11)
    return {
        "linear_query": centred(key_list[0], (CONTEXT_TOKENS, H * HD), 1.0, 6.0, ((0, 8), (1, 4))),
        "linear_key": centred(key_list[1], (CONTEXT_TOKENS, H * HD), 1.0, 6.0, ((0, 8), (1, 4))),
        "linear_value": centred(key_list[2], (CONTEXT_TOKENS, H * HD), 1.0, 6.0, ((0, 8), (1, 4))),
        "log_decay": draw_log_decay(jax.random.fold_in(key_list[10], 71), 0),
        "norm_gain": jnp.clip(1.0 + 0.15 * jax.random.normal(key_list[4], (H * HD,), jnp.float32), 0.25, 1.75),
        "soft_query": draw_soft_query(jax.random.fold_in(key_list[10], 71), 0),
        "soft_key": draw_soft_key(jax.random.fold_in(key_list[10], 71), 0),
        "soft_value": centred(key_list[7], (CONTEXT_TOKENS, H * HD), 1.0, 6.0, ((0, 8), (1, 4))),
        "block_index": draw_block_index(jax.random.fold_in(key_list[10], 71), 0),
        "block_count": draw_block_count(jax.random.fold_in(key_list[10], 71), 0),
    }


EPS = 1e-06

def rounded(matrix):
    return lax.optimization_barrier(matrix.astype(jnp.bfloat16)).astype(jnp.float32)

def causal_mask(length):
    rows_iota = lax.broadcasted_iota(jnp.int32, (length, length), 0)
    cols_iota = lax.broadcasted_iota(jnp.int32, (length, length), 1)
    return cols_iota <= rows_iota

def block_decays(decay_sec):
    per_block = decay_sec.reshape(H, SEC // BLK, BLK).transpose(1, 0, 2)
    cumulative = jnp.cumsum(per_block, axis=2)
    return (cumulative, cumulative[:, :, -1])

def state_step(carried, keys_blk, values_blk, cumul_blk, total_blk):
    keys_wide = keys_blk.astype(jnp.float32)
    values_wide = values_blk.astype(jnp.float32)
    decayed = rounded(keys_wide * jnp.exp(total_blk[:, None] - cumul_blk).T[:, :, None])
    update = jnp.einsum('jhd,jhe->hde', decayed, values_wide)
    return jnp.exp(total_blk)[:, None, None] * carried + update

def section_states(inputs):
    key_sec, value_sec, decay_sec = inputs
    cumulative, totals = block_decays(decay_sec)
    keys_blocks = key_sec.reshape(SEC // BLK, BLK, H, HD)
    values_blocks = value_sec.reshape(SEC // BLK, BLK, H, HD)

    def advance(carried, pieces):
        return (state_step(carried, pieces[0], pieces[1], pieces[2], pieces[3]), 0.0)
    start = jnp.zeros((H, HD, HD), jnp.float32)
    final, unused = lax.scan(advance, start, (keys_blocks, values_blocks, cumulative, totals))
    return (final, lax.optimization_barrier(jnp.sum(decay_sec, axis=1)))

def section_output(inputs):
    query_sec, key_sec, value_sec, decay_sec, incoming, gain = inputs
    cumulative, totals = block_decays(decay_sec)
    query_blocks = query_sec.reshape(SEC // BLK, BLK, H, HD)
    keys_blocks = key_sec.reshape(SEC // BLK, BLK, H, HD)
    values_blocks = value_sec.reshape(SEC // BLK, BLK, H, HD)
    allowed = causal_mask(BLK)

    def advance(carried, pieces):
        query_blk, keys_blk, values_blk, cumul_blk, total_blk = pieces
        query_wide = query_blk.astype(jnp.float32)
        scores = jnp.einsum('thd,jhd->htj', query_wide, keys_blk.astype(jnp.float32))
        differ = cumul_blk[:, :, None] - cumul_blk[:, None, :]
        weights = jnp.where(allowed[None], jnp.exp(jnp.minimum(differ, 0.0)), 0.0)
        inside = jnp.einsum('htj,jhd->thd', rounded(scores * weights), values_blk.astype(jnp.float32))
        decayed_query = rounded(query_wide * jnp.exp(cumul_blk).T[:, :, None])
        across = jnp.einsum('thd,hde->the', decayed_query, rounded(carried))
        following = state_step(carried, keys_blk, values_blk, cumul_blk, total_blk)
        return (following, inside + across)
    start = jnp.zeros((H, HD, HD), jnp.float32)
    final, outputs = lax.scan(advance, start, (query_blocks, keys_blocks, values_blocks, cumulative, totals))
    section_cum = jnp.cumsum(decay_sec, axis=1)
    scaled = rounded(query_sec.astype(jnp.float32) * jnp.exp(section_cum).T[:, :, None])
    raw = outputs.reshape(SEC, H, HD) + jnp.einsum('thd,hde->the', scaled, rounded(incoming))
    square_mean = lax.optimization_barrier(jnp.mean(raw * raw, axis=2, keepdims=True))
    normed = raw / jnp.sqrt(square_mean + EPS) * gain.reshape(H, HD)
    return normed.astype(jnp.bfloat16).reshape(SEC, H * HD)

def attend(query_blk, keys_sel, values_sel, index_row, count_row, row_global):
    inverse_root = 1.0 / math.sqrt(HD)
    scores = jnp.einsum('thd,kjhd->htkj', query_blk.astype(jnp.float32), keys_sel.astype(jnp.float32)) * inverse_root
    slot_used = jnp.arange(index_row.shape[0], dtype=jnp.int32) < count_row
    off_diagonal = jnp.logical_not(index_row == row_global)
    allowed = slot_used[None, :, None] & (off_diagonal[None, :, None] | causal_mask(BLK)[:, None, :])
    scores = jnp.where(allowed[None], scores, -jnp.inf)
    highest = lax.optimization_barrier(jnp.max(scores, axis=(2, 3), keepdims=True))
    raised = jnp.exp(scores - highest)
    weights = rounded(raised / lax.optimization_barrier(jnp.sum(raised, axis=(2, 3), keepdims=True)))
    output = jnp.einsum('htkj,kjhd->thd', weights, values_sel.astype(jnp.float32))
    return output.astype(jnp.bfloat16).reshape(BLK, H * HD)

def reference(linear_query, linear_key, linear_value, log_decay, norm_gain, soft_query, soft_key, soft_value, block_index, block_count):
    sections = CONTEXT_TOKENS // SEC
    query_secs = linear_query.reshape(sections, SEC, H, HD)
    key_secs = linear_key.reshape(sections, SEC, H, HD)
    value_secs = linear_value.reshape(sections, SEC, H, HD)
    decay_secs = log_decay.reshape(H, sections, SEC).transpose(1, 0, 2)
    finals, totals = lax.map(section_states, (key_secs, value_secs, decay_secs))

    def chained(carried, pieces):
        return (jnp.exp(pieces[1])[:, None, None] * carried + pieces[0], carried)
    last_state, incoming = lax.scan(chained, jnp.zeros((H, HD, HD), jnp.float32), (finals, totals))
    gains = jnp.broadcast_to(norm_gain, (sections, H * HD))
    linear_out = lax.map(section_output, (query_secs, key_secs, value_secs, decay_secs, incoming, gains))
    linear_rows = linear_out.reshape(CONTEXT_TOKENS, H * HD)
    key_blocks = soft_key.reshape(QBLOCKS, BLK, H, HD)
    value_blocks = soft_value.reshape(QBLOCKS, BLK, H, HD)
    query_blocks = soft_query.reshape(QBLOCKS, BLK, H, HD)
    rows_all = jnp.arange(QBLOCKS, dtype=jnp.int32)

    def one_block(pieces):
        query_blk, index_row, count_row, row_global = pieces
        keys_sel = jnp.take(key_blocks, index_row, axis=0)
        values_sel = jnp.take(value_blocks, index_row, axis=0)
        return attend(query_blk, keys_sel, values_sel, index_row, count_row, row_global)
    soft_out = lax.map(one_block, (query_blocks, block_index, block_count, rows_all))
    return (linear_rows, soft_out.reshape(CONTEXT_TOKENS, H * HD))
```

```python
import functools
import math

import jax
import jax.numpy as jnp
from jax import lax
from jax.experimental import pallas as pl
from jax.experimental.pallas import tpu as pltpu
from jax.sharding import PartitionSpec as P

BLK = 128
HD = 128
REACH = 4
PER_GROUP = 2
EPS = 1e-06
OFF = -1e30
F32 = jnp.float32
BF16 = jnp.bfloat16
MESH = pl.DeviceIdType.MESH
NT = (((1,), (1,)), ((), ()))
TN = (((0,), (0,)), ((), ()))


def dot(a, b):
    return jnp.dot(a, b, preferred_element_type=F32)


def kernel(sections, peers, heads,
           lq, lk, lv, ld, gain, sq, sk, sv, bias,
           out_lin, out_soft,
           ak, av, bk, bv, lstage, sstage, cc, g0s, g1s, exd, exp_, l1, fown, fsend, frecv, xsend, xrecv, inc,
           a_send, a_recv, b_send, b_recv, d_send, d_recv, f_send, f_recv, x_send, x_recv, o_send, o_recv, o_local):
    groups = heads // PER_GROUP
    wide = PER_GROUP * HD
    length = lq.shape[0]
    rows = length // peers
    c, h = lax.axis_index("ctx"), lax.axis_index("head")
    odd = lax.rem(c, 2)
    even = 1 - odd
    partner = c + 1 - 2 * odd
    after, before = lax.rem(c + 2, sections), lax.rem(c + sections - 2, sections)
    has_after, has_before = c + 2 < sections, c >= 2
    has_b = c >= 1
    sends_b = jnp.logical_or(odd == 0, has_before)

    def cols(g):
        return pl.ds(pl.multiple_of(g * wide, wide), wide)

    def hcols(i):
        return pl.ds(pl.multiple_of(i * HD, HD), HD)

    def remote(src, dst, send, recv, where):
        return pltpu.make_async_remote_copy(
            src_ref=src, dst_ref=dst, send_sem=send, recv_sem=recv, device_id=where, device_id_type=MESH)

    def copies_a(g):
        return [remote(src.at[:, cols(g)], dst.at[:, cols(g)], a_send.at[n, g], a_recv.at[n, g], {"ctx": after})
                for n, (src, dst) in enumerate(((sk, ak), (sv, av)))]

    def copies_b(g, sources):
        return [remote(src.at[:, cols(g)], dst.at[:, cols(g)], b_send.at[n, g], b_recv.at[n, g], {"ctx": partner})
                for n, (src, dst) in enumerate(zip(sources, (bk, bv)))]

    def hd(g):
        return pl.ds(g * PER_GROUP, PER_GROUP)

    def copy_f(g):
        return remote(fsend.at[hd(g)], frecv.at[hd(g)], f_send.at[g], f_recv.at[g], {"ctx": partner})

    def copy_x(g):
        return remote(xsend.at[hd(g)], xrecv.at[hd(g)], x_send.at[g], x_recv.at[g], {"ctx": after})

    copy_d = remote(exd, exp_, d_send, d_recv, {"ctx": partner})

    def out_cols(g):
        return pl.ds(pl.multiple_of(h * (heads * HD) + g * wide, wide), wide)

    def copies_out(n, stage, out, g):
        made = []
        for k in range(1, peers):
            to = lax.rem(h + k, peers)
            made.append(remote(stage.at[pl.ds(pl.multiple_of(to * rows, rows), rows), cols(g)],
                               out.at[:, out_cols(g)],
                               o_send.at[n, g, k - 1], o_recv.at[n, g, k - 1], {"head": to}))
        return made

    def copy_local(n, stage, out, g):
        return pltpu.make_async_copy(stage.at[pl.ds(pl.multiple_of(h * rows, rows), rows), cols(g)],
                                     out.at[:, out_cols(g)], o_local.at[n, g])

    barrier = pltpu.get_barrier_semaphore()
    pl.semaphore_signal(barrier, inc=1, device_id={"ctx": partner}, device_id_type=MESH)
    for k in range(1, peers):
        pl.semaphore_signal(barrier, inc=1, device_id={"head": lax.rem(h + k, peers)}, device_id_type=MESH)

    @pl.when(has_after)
    def _():
        pl.semaphore_signal(barrier, inc=1, device_id={"ctx": after}, device_id_type=MESH)

    @pl.when(has_before)
    def _():
        pl.semaphore_signal(barrier, inc=1, device_id={"ctx": before}, device_id_type=MESH)

    pl.semaphore_wait(barrier, peers + has_after.astype(jnp.int32) + has_before.astype(jnp.int32))

    def start_kv(g, carry):
        @pl.when(has_after)
        def _():
            for copy in copies_a(g):
                copy.start()

        @pl.when(odd == 0)
        def _():
            for copy in copies_b(g, (sk, sv)):
                copy.start()
        return carry

    lax.fori_loop(0, groups, start_kv, 0)

    lane = lax.broadcasted_iota(jnp.int32, (heads, length), 1)
    total = ld[...]
    for shift in (1, 2, 4, 8, 16, 32, 64):
        total = total + jnp.where(lax.rem(lane, BLK) >= shift, pltpu.roll(total, shift, 1), 0.0)
    first = jnp.broadcast_to(total[:, BLK - 1:BLK], (heads, HD))
    second = jnp.broadcast_to(total[:, 2 * BLK - 1:2 * BLK], (heads, HD))
    whole = jnp.exp(first + second)
    for i in range(heads):
        cc[i] = total[i:i + 1]
        g0s[i] = first[i:i + 1]
        g1s[i] = second[i:i + 1]
        exd[i] = jnp.broadcast_to(whole[i:i + 1], (8, HD))
    copy_d.start()

    def columns_of(i, b):
        along = jnp.broadcast_to(cc[i, :, pl.ds(b * BLK, BLK)], (BLK, BLK))
        return along, along.T

    def states(g, carry):
        for n in range(PER_GROUP):
            i = g * PER_GROUP + n
            ends = (g0s[i], g1s[i])
            update = []
            for b in range(2):
                along, down = columns_of(i, b)
                part = pl.ds(b * BLK, BLK)
                kc = (lk[part, hcols(i)].astype(F32) * jnp.exp(ends[b] - down)).astype(BF16)
                update.append(lax.dot_general(kc, lv[part, hcols(i)], TN, preferred_element_type=F32))
            final = jnp.exp(ends[1]) * update[0] + update[1]
            l1[i] = update[0].astype(BF16)
            fown[i] = final
            fsend[i] = final.astype(BF16)
        copy_f(g).start()
        return carry

    lax.fori_loop(0, groups, states, 0)

    @pl.when(c < 2)
    def _():
        ak[...] = jnp.zeros_like(ak)
        av[...] = jnp.zeros_like(av)
        xrecv[...] = jnp.zeros_like(xrecv)

    @pl.when(c < 1)
    def _():
        bk[...] = jnp.zeros_like(bk)
        bv[...] = jnp.zeros_like(bv)

    copy_d.wait()
    r_iota = lax.broadcasted_iota(jnp.int32, (BLK, BLK), 0)
    c_iota = lax.broadcasted_iota(jnp.int32, (BLK, BLK), 1)
    scale = 1.0 / math.sqrt(HD)

    def forward(g):
        @pl.when(has_before)
        def _():
            for copy in copies_a(g):
                copy.wait_recv()

        @pl.when(jnp.logical_and(odd == 1, has_before))
        def _():
            for copy in copies_b(g, (ak, av)):
                copy.start()

    def chain(g):
        copy_f(g).wait_recv()

        @pl.when(has_before)
        def _():
            copy_x(g).wait_recv()

        for n in range(PER_GROUP):
            i = g * PER_GROUP + n
            mine, other, x = fown[i], frecv[i].astype(F32), xrecv[i].astype(F32)
            d_mine, d_other = exd[i][:1], exp_[i][:1]
            is_odd = odd == 1
            mid = jnp.where(is_odd, d_other, d_mine) * x + jnp.where(is_odd, other, mine)
            xsend[i] = (jnp.where(is_odd, d_mine, d_other) * mid + jnp.where(is_odd, mine, other)).astype(xsend.dtype)
            inc[i] = jnp.where(is_odd, mid, x).astype(BF16)

        @pl.when(has_after)
        def _():
            copy_x(g).start()

    def softmax(g):
        @pl.when(has_b)
        def _():
            for copy in copies_b(g, (sk, sv)):
                copy.wait_recv()

        causal = c_iota <= r_iota
        for n in range(PER_GROUP):
            i = g * PER_GROUP + n
            kw = jnp.concatenate([ak[:, hcols(i)], bk[:, hcols(i)], sk[:, hcols(i)]], axis=0)
            vw = jnp.concatenate([av[:, hcols(i)], bv[:, hcols(i)], sv[:, hcols(i)]], axis=0)
            for b in range(2):
                part = pl.ds(b * BLK, BLK)
                span = slice(b * BLK, b * BLK + (REACH + 1) * BLK)
                s = lax.dot_general(sq[part, hcols(i)], kw[span], NT, preferred_element_type=F32) * scale
                s = jnp.concatenate([s[:, :REACH * BLK] + bias[b:b + 1, :],
                                     jnp.where(causal, s[:, REACH * BLK:], OFF)], axis=1)
                p = jnp.exp(s - jnp.max(s, axis=1, keepdims=True))
                w = (p * (1.0 / jnp.sum(p, axis=1, keepdims=True))).astype(BF16)
                sstage[part, hcols(i)] = dot(w, vw[span]).astype(BF16)
        for copy in copies_out(1, sstage, out_soft, g):
            copy.start()
        copy_local(1, sstage, out_soft, g).start()

    def linear(g):
        causal = c_iota <= r_iota
        for n in range(PER_GROUP):
            i = g * PER_GROUP + n
            incoming = inc[i]
            for b in range(2):
                part = pl.ds(b * BLK, BLK)
                along, down = columns_of(i, b)
                q, k, v = lq[part, hcols(i)], lk[part, hcols(i)], lv[part, hcols(i)]
                s = lax.dot_general(q, k, NT, preferred_element_type=F32)
                s = s * jnp.where(causal, jnp.exp(jnp.minimum(down - along, 0.0)), 0.0)
                raw = dot(s.astype(BF16), v)
                wide_q = q.astype(F32)
                if b == 0:
                    raw += dot((wide_q * jnp.exp(down)).astype(BF16), incoming)
                else:
                    raw += dot((wide_q * jnp.exp(down)).astype(BF16), l1[i])
                    raw += dot((wide_q * jnp.exp(down + g0s[i])).astype(BF16), incoming)
                square = jnp.mean(raw * raw, axis=1, keepdims=True)
                lstage[part, hcols(i)] = (raw * lax.rsqrt(square + EPS) * gain[:, hcols(i)]).astype(BF16)
        for copy in copies_out(0, lstage, out_lin, g):
            copy.start()
        copy_local(0, lstage, out_lin, g).start()

    forward(0)

    def main(g, carry):
        chain(g)

        @pl.when(g + 1 < groups)
        def _():
            forward(g + 1)
        softmax(g)
        linear(g)
        return carry

    lax.fori_loop(0, groups, main, 0)

    def finish(g, carry):
        @pl.when(has_after)
        def _():
            for copy in copies_a(g):
                copy.wait_send()
            copy_x(g).wait_send()

        @pl.when(sends_b)
        def _():
            for copy in copies_b(g, (sk, sv)):
                copy.wait_send()
        copy_f(g).wait_send()
        for n, (stage, out) in enumerate(((lstage, out_lin), (sstage, out_soft))):
            copy_local(n, stage, out, g).wait()
            for copy in copies_out(n, stage, out, g):
                copy.wait()
        return carry

    lax.fori_loop(0, groups, finish, 0)


def local(sections, peers, linear_query, linear_key, linear_value, log_decay, norm_gain,
          soft_query, soft_key, soft_value, block_index, block_count):
    heads, length = log_decay.shape
    width = linear_query.shape[1]
    groups = heads // PER_GROUP
    here = length // BLK
    own = lax.axis_index("ctx") * here + jnp.arange(here, dtype=jnp.int32)
    named = own[:, None] - REACH + jnp.arange(REACH, dtype=jnp.int32)[None, :]
    used = jnp.arange(block_index.shape[1], dtype=jnp.int32)[None, :] < block_count[:, None]
    seen = jnp.any(used[:, None, :] & (block_index[:, None, :] == named[:, :, None]), axis=2)
    bias = jnp.repeat(jnp.where(seen, 0.0, OFF).astype(F32), BLK, axis=1)
    carried = BF16 if sections <= 8 else F32
    vmem = pl.BlockSpec(memory_space=pltpu.VMEM)
    rows = length // peers
    state = (heads, HD, HD)
    dma = pltpu.SemaphoreType.DMA
    return pl.pallas_call(
        functools.partial(kernel, sections, peers, heads),
        out_shape=[jax.ShapeDtypeStruct((rows, width * peers), BF16)] * 2,
        in_specs=[vmem] * 9,
        out_specs=[pl.BlockSpec(memory_space=pl.ANY)] * 2,
        scratch_shapes=[pltpu.VMEM((length, width), BF16)] * 6 + [
            pltpu.VMEM((heads, 1, length), F32),
            pltpu.VMEM((heads, 1, HD), F32),
            pltpu.VMEM((heads, 1, HD), F32),
            pltpu.VMEM((heads, 8, HD), F32),
            pltpu.VMEM((heads, 8, HD), F32),
            pltpu.VMEM(state, BF16),
            pltpu.VMEM(state, F32),
            pltpu.VMEM(state, BF16),
            pltpu.VMEM(state, BF16),
            pltpu.VMEM(state, carried),
            pltpu.VMEM(state, carried),
            pltpu.VMEM(state, BF16),
            dma((2, groups)), dma((2, groups)), dma((2, groups)), dma((2, groups)),
            dma, dma, dma((groups,)), dma((groups,)), dma((groups,)), dma((groups,)),
            dma((2, groups, peers - 1)), dma((2, groups, peers - 1)), dma((2, groups)),
        ],
        compiler_params=pltpu.CompilerParams(
            collective_id=0, has_side_effects=True, vmem_limit_bytes=48 * 1024 * 1024),
        cost_estimate=pl.CostEstimate(flops=2_400_000_000, bytes_accessed=10_000_000, transcendentals=4_000_000),
    )(linear_query, linear_key, linear_value, log_decay, norm_gain.reshape(1, width),
      soft_query, soft_key, soft_value, bias)


def solution(mesh):
    in_specs = (
        P("ctx", "head"), P("ctx", "head"), P("ctx", "head"), P("head", "ctx"), P("head"),
        P("ctx", "head"), P("ctx", "head"), P("ctx", "head"), P("ctx", None), P("ctx"),
    )
    out_specs = (P(("ctx", "head"), None), P(("ctx", "head"), None))
    body = functools.partial(local, mesh.shape["ctx"], mesh.shape["head"])
    return jax.shard_map(body, mesh=mesh, in_specs=in_specs, out_specs=out_specs, check_vma=False)
```

```python
import functools
import math

import jax
import jax.numpy as jnp
from jax import lax
from jax.experimental import pallas as pl
from jax.experimental.pallas import tpu as pltpu
from jax.sharding import PartitionSpec as P

BLK = 128
HD = 128
REACH = 4
PER_GROUP = 2
AHEAD = 3
EPS = 1e-06
OFF = -1e30
F32 = jnp.float32
BF16 = jnp.bfloat16
MESH = pl.DeviceIdType.MESH
NT = (((1,), (1,)), ((), ()))
TN = (((0,), (0,)), ((), ()))


def dot(a, b):
    return jnp.dot(a, b, preferred_element_type=F32)


def kernel(sections, peers, heads,
           lq_hbm, lk_hbm, lv_hbm, ld, gain, sq_hbm, sk_hbm, sv_hbm, bias,
           out_lin, out_soft,
           lq, lk, lv, sq, sk, sv, ak, av, bk, bv, lstage, sstage,
           cc, last, exd, exp_, fown, fsend, frecv, xsend, xrecv, inc, load,
           a_send, a_recv, b_send, b_recv, d_send, d_recv, f_send, f_recv, x_send, x_recv, o_send, o_recv, o_local):
    groups = heads // PER_GROUP
    wide = PER_GROUP * HD
    length = lq_hbm.shape[0]
    rows = length // peers
    c, h = lax.axis_index("ctx"), lax.axis_index("head")
    odd = lax.rem(c, 2)
    even = 1 - odd
    partner = c + 1 - 2 * odd
    after, before = lax.rem(c + 2, sections), lax.rem(c + sections - 2, sections)
    has_after, has_before = c + 2 < sections, c >= 2
    has_b = c >= 1
    sends_b = jnp.logical_or(odd == 0, has_before)

    def cols(g):
        return pl.ds(pl.multiple_of(g * wide, wide), wide)

    def hcols(i):
        return pl.ds(pl.multiple_of(i * HD, HD), HD)

    def remote(src, dst, send, recv, where):
        return pltpu.make_async_remote_copy(
            src_ref=src, dst_ref=dst, send_sem=send, recv_sem=recv, device_id=where, device_id_type=MESH)

    def copies_a(g):
        return [remote(src.at[:, cols(g)], dst.at[:, cols(g)], a_send.at[n, g], a_recv.at[n, g], {"ctx": after})
                for n, (src, dst) in enumerate(((sk_hbm, ak), (sv_hbm, av)))]

    def copies_b(g, sources):
        return [remote(src.at[:, cols(g)], dst.at[:, cols(g)], b_send.at[n, g], b_recv.at[n, g], {"ctx": partner})
                for n, (src, dst) in enumerate(zip(sources, (bk, bv)))]

    def hd(g):
        return pl.ds(g * PER_GROUP, PER_GROUP)

    def copy_f(g):
        return remote(fsend.at[hd(g)], frecv.at[hd(g)], f_send.at[g], f_recv.at[g], {"ctx": partner})

    def copy_x(g):
        return remote(xsend.at[hd(g)], xrecv.at[hd(g)], x_send.at[g], x_recv.at[g], {"ctx": after})

    copy_d = remote(exd, exp_, d_send, d_recv, {"ctx": partner})

    def out_cols(g):
        return pl.ds(pl.multiple_of(h * (heads * HD) + g * wide, wide), wide)

    def copies_out(n, stage, out, g):
        made = []
        for k in range(1, peers):
            to = lax.rem(h + k, peers)
            made.append(remote(stage.at[pl.ds(pl.multiple_of(to * rows, rows), rows), cols(g)],
                               out.at[:, out_cols(g)],
                               o_send.at[n, g, k - 1], o_recv.at[n, g, k - 1], {"head": to}))
        return made

    def copy_local(n, stage, out, g):
        return pltpu.make_async_copy(stage.at[pl.ds(pl.multiple_of(h * rows, rows), rows), cols(g)],
                                     out.at[:, out_cols(g)], o_local.at[n, g])

    loads = [pltpu.make_async_copy(src, dst, load.at[n]) for n, (src, dst) in enumerate(
        ((lk_hbm, lk), (lv_hbm, lv), (lq_hbm, lq), (sq_hbm, sq), (sk_hbm, sk), (sv_hbm, sv)))]
    for copy in loads:
        copy.start()

    barrier = pltpu.get_barrier_semaphore()
    pl.semaphore_signal(barrier, inc=1, device_id={"ctx": partner}, device_id_type=MESH)
    for k in range(1, peers):
        pl.semaphore_signal(barrier, inc=1, device_id={"head": lax.rem(h + k, peers)}, device_id_type=MESH)

    @pl.when(has_after)
    def _():
        pl.semaphore_signal(barrier, inc=1, device_id={"ctx": after}, device_id_type=MESH)

    @pl.when(has_before)
    def _():
        pl.semaphore_signal(barrier, inc=1, device_id={"ctx": before}, device_id_type=MESH)

    pl.semaphore_wait(barrier, peers + has_after.astype(jnp.int32) + has_before.astype(jnp.int32))

    def start_kv(g):
        @pl.when(has_after)
        def _():
            for copy in copies_a(g):
                copy.start()

        @pl.when(odd == 0)
        def _():
            for copy in copies_b(g, (sk_hbm, sv_hbm)):
                copy.start()

    for g in range(AHEAD):
        start_kv(g)

    lane = lax.broadcasted_iota(jnp.int32, (heads, length), 1)
    total = ld[...]
    shift = 1
    while shift < length:
        total = total + jnp.where(lane >= shift, pltpu.roll(total, shift, 1), 0.0)
        shift *= 2
    ends = jnp.broadcast_to(total[:, length - 1:], (heads, HD))
    whole = jnp.exp(ends)
    for i in range(heads):
        cc[i] = total[i:i + 1]
        last[i] = ends[i:i + 1]
        exd[i] = jnp.broadcast_to(whole[i:i + 1], (8, HD))
    copy_d.start()

    def columns_of(i):
        along = [jnp.broadcast_to(cc[i, :, pl.ds(b * BLK, BLK)], (BLK, BLK)) for b in range(2)]
        return along, [part.T for part in along]

    for n in (0, 1):
        loads[n].wait()

    def states(g, carry):
        for n in range(PER_GROUP):
            i = g * PER_GROUP + n
            down = jnp.concatenate(columns_of(i)[1], axis=0)
            kc = (lk[:, hcols(i)].astype(F32) * jnp.exp(last[i] - down)).astype(BF16)
            final = lax.dot_general(kc, lv[:, hcols(i)], TN, preferred_element_type=F32)
            fown[i] = final
            fsend[i] = final.astype(BF16)
        copy_f(g).start()
        return carry

    lax.fori_loop(0, groups, states, 0)

    @pl.when(c < 2)
    def _():
        ak[...] = jnp.zeros_like(ak)
        av[...] = jnp.zeros_like(av)
        xrecv[...] = jnp.zeros_like(xrecv)

    @pl.when(c < 1)
    def _():
        bk[...] = jnp.zeros_like(bk)
        bv[...] = jnp.zeros_like(bv)

    copy_d.wait()
    for n in range(2, 6):
        loads[n].wait()
    r_iota = lax.broadcasted_iota(jnp.int32, (BLK, BLK), 0)
    c_iota = lax.broadcasted_iota(jnp.int32, (BLK, BLK), 1)
    scale = math.log2(math.e) / math.sqrt(HD)

    def forward(g):
        @pl.when(has_before)
        def _():
            for copy in copies_a(g):
                copy.wait_recv()

        @pl.when(jnp.logical_and(odd == 1, has_before))
        def _():
            for copy in copies_b(g, (ak, av)):
                copy.start()

    def chain(g):
        copy_f(g).wait_recv()

        @pl.when(has_before)
        def _():
            copy_x(g).wait_recv()

        for n in range(PER_GROUP):
            i = g * PER_GROUP + n
            mine, other, x = fown[i], frecv[i].astype(F32), xrecv[i].astype(F32)
            d_mine, d_other = exd[i][:1], exp_[i][:1]
            is_odd = odd == 1
            mid = jnp.where(is_odd, d_other, d_mine) * x + jnp.where(is_odd, other, mine)
            xsend[i] = (jnp.where(is_odd, d_mine, d_other) * mid + jnp.where(is_odd, mine, other)).astype(xsend.dtype)
            inc[i] = jnp.where(is_odd, mid, x).astype(BF16)

        @pl.when(has_after)
        def _():
            copy_x(g).start()

    def softmax(g):
        @pl.when(has_b)
        def _():
            for copy in copies_b(g, (sk_hbm, sv_hbm)):
                copy.wait_recv()

        causal = c_iota <= r_iota
        mine = [g * PER_GROUP + n for n in range(PER_GROUP)]
        scores = []
        for i in mine:
            kw = jnp.concatenate([ak[:, hcols(i)], bk[:, hcols(i)], sk[:, hcols(i)]], axis=0)
            scores.append(lax.dot_general(sq[:, hcols(i)], kw, NT, preferred_element_type=F32))
        weights, sums = [], []
        none = jnp.zeros((BLK, BLK), BF16)
        for whole_s in scores:
            parts, inverse = [], []
            for b in range(2):
                s = whole_s[b * BLK:(b + 1) * BLK, b * BLK:(b + REACH + 1) * BLK] * scale
                s = jnp.concatenate([s[:, :REACH * BLK] + bias[b:b + 1, :],
                                     jnp.where(causal, s[:, REACH * BLK:], OFF)], axis=1)
                p = jnp.exp2(s - jnp.max(s, axis=1, keepdims=True))
                inverse.append(1.0 / jnp.sum(p, axis=1, keepdims=True))
                p = p.astype(BF16)
                parts.append(jnp.concatenate([p, none] if b == 0 else [none, p], axis=1))
            weights.append(jnp.concatenate(parts, axis=0))
            sums.append(jnp.concatenate(inverse, axis=0))
        for i, w, inverse in zip(mine, weights, sums):
            vw = jnp.concatenate([av[:, hcols(i)], bv[:, hcols(i)], sv[:, hcols(i)]], axis=0)
            sstage[:, hcols(i)] = (dot(w, vw) * inverse).astype(BF16)
        for copy in copies_out(1, sstage, out_soft, g):
            copy.start()
        copy_local(1, sstage, out_soft, g).start()

    def linear(g):
        causal = c_iota <= r_iota
        mine = [g * PER_GROUP + n for n in range(PER_GROUP)]
        none = jnp.zeros((BLK, BLK), BF16)
        scores = [lax.dot_general(lq[:, hcols(i)], lk[:, hcols(i)], NT, preferred_element_type=F32) for i in mine]
        left = []
        for i, s in zip(mine, scores):
            along, down = columns_of(i)
            top = s[:BLK, :BLK] * jnp.where(causal, jnp.exp(down[0] - along[0]), 0.0)
            across = s[BLK:, :BLK] * jnp.exp(down[1] - along[0])
            low = s[BLK:, BLK:] * jnp.where(causal, jnp.exp(down[1] - along[1]), 0.0)
            decayed = (lq[:, hcols(i)].astype(F32) * jnp.exp(jnp.concatenate(down, axis=0))).astype(BF16)
            left.append(jnp.concatenate([
                jnp.concatenate([top.astype(BF16), none], axis=1),
                jnp.concatenate([across.astype(BF16), low.astype(BF16)], axis=1)], axis=0))
            left[-1] = jnp.concatenate([left[-1], decayed], axis=1)
        for i, p in zip(mine, left):
            raw = dot(p, jnp.concatenate([lv[:, hcols(i)], inc[i]], axis=0))
            square = jnp.mean(raw * raw, axis=1, keepdims=True)
            lstage[:, hcols(i)] = (raw * lax.rsqrt(square + EPS) * gain[:, hcols(i)]).astype(BF16)
        for copy in copies_out(0, lstage, out_lin, g):
            copy.start()
        copy_local(0, lstage, out_lin, g).start()

    forward(0)

    def main(g, carry):
        chain(g)

        @pl.when(g + AHEAD < groups)
        def _():
            start_kv(g + AHEAD)
        linear(g)

        @pl.when(g + 1 < groups)
        def _():
            forward(g + 1)
        softmax(g)
        return carry

    lax.fori_loop(0, groups, main, 0)

    def finish(g, carry):
        @pl.when(has_after)
        def _():
            for copy in copies_a(g):
                copy.wait_send()
            copy_x(g).wait_send()

        @pl.when(sends_b)
        def _():
            for copy in copies_b(g, (sk_hbm, sv_hbm)):
                copy.wait_send()
        copy_f(g).wait_send()
        for n, (stage, out) in enumerate(((lstage, out_lin), (sstage, out_soft))):
            copy_local(n, stage, out, g).wait()
            for copy in copies_out(n, stage, out, g):
                copy.wait()
        return carry

    lax.fori_loop(0, groups, finish, 0)


def local(sections, peers, linear_query, linear_key, linear_value, log_decay, norm_gain,
          soft_query, soft_key, soft_value, block_index, block_count):
    heads, length = log_decay.shape
    width = linear_query.shape[1]
    groups = heads // PER_GROUP
    here = length // BLK
    own = lax.axis_index("ctx") * here + jnp.arange(here, dtype=jnp.int32)
    named = own[:, None] - REACH + jnp.arange(REACH, dtype=jnp.int32)[None, :]
    used = jnp.arange(block_index.shape[1], dtype=jnp.int32)[None, :] < block_count[:, None]
    seen = jnp.any(used[:, None, :] & (block_index[:, None, :] == named[:, :, None]), axis=2)
    bias = jnp.repeat(jnp.where(seen, 0.0, OFF).astype(F32), BLK, axis=1)
    carried = BF16 if sections <= 8 else F32
    vmem, hbm = pl.BlockSpec(memory_space=pltpu.VMEM), pl.BlockSpec(memory_space=pl.ANY)
    rows = length // peers
    state = (heads, HD, HD)
    dma = pltpu.SemaphoreType.DMA
    return pl.pallas_call(
        functools.partial(kernel, sections, peers, heads),
        out_shape=[jax.ShapeDtypeStruct((rows, width * peers), BF16)] * 2,
        in_specs=[hbm, hbm, hbm, vmem, vmem, hbm, hbm, hbm, vmem],
        out_specs=[hbm] * 2,
        scratch_shapes=[pltpu.VMEM((length, width), BF16)] * 12 + [
            pltpu.VMEM((heads, 1, length), F32),
            pltpu.VMEM((heads, 1, HD), F32),
            pltpu.VMEM((heads, 8, HD), F32),
            pltpu.VMEM((heads, 8, HD), F32),
            pltpu.VMEM(state, F32),
            pltpu.VMEM(state, BF16),
            pltpu.VMEM(state, BF16),
            pltpu.VMEM(state, carried),
            pltpu.VMEM(state, carried),
            pltpu.VMEM(state, BF16),
            dma((6,)), dma((2, groups)), dma((2, groups)), dma((2, groups)), dma((2, groups)),
            dma, dma, dma((groups,)), dma((groups,)), dma((groups,)), dma((groups,)),
            dma((2, groups, peers - 1)), dma((2, groups, peers - 1)), dma((2, groups)),
        ],
        compiler_params=pltpu.CompilerParams(
            collective_id=0, has_side_effects=True, vmem_limit_bytes=60 * 1024 * 1024),
        cost_estimate=pl.CostEstimate(flops=2_400_000_000, bytes_accessed=10_000_000, transcendentals=4_000_000),
    )(linear_query, linear_key, linear_value, log_decay, norm_gain.reshape(1, width),
      soft_query, soft_key, soft_value, bias)


def solution(mesh):
    in_specs = (
        P("ctx", "head"), P("ctx", "head"), P("ctx", "head"), P("head", "ctx"), P("head"),
        P("ctx", "head"), P("ctx", "head"), P("ctx", "head"), P("ctx", None), P("ctx"),
    )
    out_specs = (P(("ctx", "head"), None), P(("ctx", "head"), None))
    body = functools.partial(local, mesh.shape["ctx"], mesh.shape["head"])
    return jax.shard_map(body, mesh=mesh, in_specs=in_specs, out_specs=out_specs, check_vma=False)
```

```python
import functools
import math

import jax
import jax.numpy as jnp
from jax import lax
from jax.experimental import pallas as pl
from jax.experimental.pallas import tpu as pltpu
from jax.sharding import PartitionSpec as P

BLK = 128
HD = 128
REACH = 4
PER_GROUP = 2
AHEAD = 4
RATE = 2
EPS = 1e-06
OFF = -1e30
F32 = jnp.float32
BF16 = jnp.bfloat16
MESH = pl.DeviceIdType.MESH
NT = (((1,), (1,)), ((), ()))
TN = (((0,), (0,)), ((), ()))


def dot(a, b):
    return jnp.dot(a, b, preferred_element_type=F32)


def kernel(sections, peers, heads,
           lq_hbm, lk_hbm, lv_hbm, ld_hbm, gain_hbm, sq_hbm, sk_hbm, sv_hbm, index, count,
           out_lin, out_soft,
           lq, lk, lv, sq, sk, sv, ak, av, bk, bv, lstage, sstage, ld, gain, bias,
           cc, last, exd, exp_, fown, fsend, frecv, xsend, xrecv, inc, load,
           a_send, a_recv, b_send, b_recv, d_send, d_recv, f_send, f_recv, x_send, x_recv, o_send, o_recv, o_local):
    groups = heads // PER_GROUP
    wide = PER_GROUP * HD
    length = lq_hbm.shape[0]
    rows = length // peers
    c, h = lax.axis_index("ctx"), lax.axis_index("head")
    odd = lax.rem(c, 2)
    even = 1 - odd
    partner = c + 1 - 2 * odd
    after, before = lax.rem(c + 2, sections), lax.rem(c + sections - 2, sections)
    has_after, has_before = c + 2 < sections, c >= 2
    has_b = c >= 1
    sends_b = jnp.logical_or(odd == 0, has_before)

    def cols(g):
        return pl.ds(pl.multiple_of(g * wide, wide), wide)

    def hcols(i):
        return pl.ds(pl.multiple_of(i * HD, HD), HD)

    def remote(src, dst, send, recv, where):
        return pltpu.make_async_remote_copy(
            src_ref=src, dst_ref=dst, send_sem=send, recv_sem=recv, device_id=where, device_id_type=MESH)

    def copies_a(g):
        return [remote(src.at[:, cols(g)], dst.at[:, cols(g)], a_send.at[n, g], a_recv.at[n, g], {"ctx": after})
                for n, (src, dst) in enumerate(((sk_hbm, ak), (sv_hbm, av)))]

    def copies_b(g, sources):
        return [remote(src.at[:, cols(g)], dst.at[:, cols(g)], b_send.at[n, g], b_recv.at[n, g], {"ctx": partner})
                for n, (src, dst) in enumerate(zip(sources, (bk, bv)))]

    def hd(g):
        return pl.ds(g * PER_GROUP, PER_GROUP)

    def copy_f(g):
        return remote(fsend.at[hd(g)], frecv.at[hd(g)], f_send.at[g], f_recv.at[g], {"ctx": partner})

    def copy_x(g):
        return remote(xsend.at[hd(g)], xrecv.at[hd(g)], x_send.at[g], x_recv.at[g], {"ctx": after})

    copy_d = remote(exd, exp_, d_send, d_recv, {"ctx": partner})

    def out_cols(g):
        return pl.ds(pl.multiple_of(h * (heads * HD) + g * wide, wide), wide)

    def copies_out(n, stage, out, g):
        made = []
        for k in range(1, peers):
            to = lax.rem(h + k, peers)
            made.append(remote(stage.at[pl.ds(pl.multiple_of(to * rows, rows), rows), cols(g)],
                               out.at[:, out_cols(g)],
                               o_send.at[n, g, k - 1], o_recv.at[n, g, k - 1], {"head": to}))
        return made

    def copy_local(n, stage, out, g):
        return pltpu.make_async_copy(stage.at[pl.ds(pl.multiple_of(h * rows, rows), rows), cols(g)],
                                     out.at[:, out_cols(g)], o_local.at[n, g])

    loads = [pltpu.make_async_copy(src, dst, load.at[n]) for n, (src, dst) in enumerate(
        ((lk_hbm, lk), (lv_hbm, lv), (lq_hbm, lq), (sq_hbm, sq), (sk_hbm, sk), (sv_hbm, sv),
         (ld_hbm, ld), (gain_hbm, gain)))]
    for n in (6, 7, 0, 1, 2, 3, 4, 5):
        loads[n].start()

    barrier = pltpu.get_barrier_semaphore()
    pl.semaphore_signal(barrier, inc=1, device_id={"ctx": partner}, device_id_type=MESH)
    for k in range(1, peers):
        pl.semaphore_signal(barrier, inc=1, device_id={"head": lax.rem(h + k, peers)}, device_id_type=MESH)

    @pl.when(has_after)
    def _():
        pl.semaphore_signal(barrier, inc=1, device_id={"ctx": after}, device_id_type=MESH)

    @pl.when(has_before)
    def _():
        pl.semaphore_signal(barrier, inc=1, device_id={"ctx": before}, device_id_type=MESH)

    pl.semaphore_wait(barrier, peers + has_after.astype(jnp.int32) + has_before.astype(jnp.int32))

    def start_kv(g):
        @pl.when(has_after)
        def _():
            for copy in copies_a(g):
                copy.start()

        @pl.when(odd == 0)
        def _():
            for copy in copies_b(g, (sk_hbm, sv_hbm)):
                copy.start()

    start_kv(0)
    for n in (6, 7):
        loads[n].wait()
    lane = lax.broadcasted_iota(jnp.int32, (heads, length), 1)
    total = ld[...]
    shift = 1
    while shift < length:
        total = total + jnp.where(lane >= shift, pltpu.roll(total, shift, 1), 0.0)
        shift *= 2
    ends = jnp.broadcast_to(total[:, length - 1:], (heads, HD))
    whole = jnp.exp(ends)
    for i in range(heads):
        cc[i] = total[i:i + 1]
        last[i] = ends[i:i + 1]
        exd[i] = jnp.broadcast_to(whole[i:i + 1], (8, HD))
    copy_d.start()

    def columns_of(i):
        along = [jnp.broadcast_to(cc[i, :, pl.ds(b * BLK, BLK)], (BLK, BLK)) for b in range(2)]
        return along, [part.T for part in along]

    for n in (0, 1):
        loads[n].wait()

    def states(g, carry):
        for n in range(PER_GROUP):
            i = g * PER_GROUP + n
            down = jnp.concatenate(columns_of(i)[1], axis=0)
            kc = (lk[:, hcols(i)].astype(F32) * jnp.exp(last[i] - down)).astype(BF16)
            final = lax.dot_general(kc, lv[:, hcols(i)], TN, preferred_element_type=F32)
            fown[i] = final
            fsend[i] = final.astype(BF16)
        copy_f(g).start()

        @pl.when(g + 1 < AHEAD)
        def _():
            start_kv(g + 1)
        return carry

    lax.fori_loop(0, groups, states, 0)

    @pl.when(c < 2)
    def _():
        ak[...] = jnp.zeros_like(ak)
        av[...] = jnp.zeros_like(av)
        xrecv[...] = jnp.zeros_like(xrecv)

    @pl.when(c < 1)
    def _():
        bk[...] = jnp.zeros_like(bk)
        bv[...] = jnp.zeros_like(bv)

    copy_d.wait()
    here = length // BLK
    for b in range(here):
        tiles = []
        for w in range(REACH):
            block = here * c + b - REACH + w
            seen = [jnp.logical_and(slot < count[b], index[b, slot] == block) for slot in range(index.shape[1])]
            tiles.append(jnp.full((1, BLK), jnp.where(functools.reduce(jnp.logical_or, seen), 0.0, OFF), F32))
        bias[b:b + 1, :] = jnp.concatenate(tiles, axis=1)
    for n in range(2, 6):
        loads[n].wait()
    r_iota = lax.broadcasted_iota(jnp.int32, (BLK, BLK), 0)
    c_iota = lax.broadcasted_iota(jnp.int32, (BLK, BLK), 1)
    scale = math.log2(math.e) / math.sqrt(HD)

    def forward(g):
        @pl.when(has_before)
        def _():
            for copy in copies_a(g):
                copy.wait_recv()

        @pl.when(jnp.logical_and(odd == 1, has_before))
        def _():
            for copy in copies_b(g, (ak, av)):
                copy.start()

    def chain(g):
        copy_f(g).wait_recv()

        @pl.when(has_before)
        def _():
            copy_x(g).wait_recv()

        for n in range(PER_GROUP):
            i = g * PER_GROUP + n
            mine, other, x = fown[i], frecv[i].astype(F32), xrecv[i].astype(F32)
            d_mine, d_other = exd[i][:1], exp_[i][:1]
            is_odd = odd == 1
            mid = jnp.where(is_odd, d_other, d_mine) * x + jnp.where(is_odd, other, mine)
            xsend[i] = (jnp.where(is_odd, d_mine, d_other) * mid + jnp.where(is_odd, mine, other)).astype(xsend.dtype)
            inc[i] = jnp.where(is_odd, mid, x).astype(BF16)

        @pl.when(has_after)
        def _():
            copy_x(g).start()

    def softmax(g):
        @pl.when(has_b)
        def _():
            for copy in copies_b(g, (sk_hbm, sv_hbm)):
                copy.wait_recv()

        causal = c_iota <= r_iota
        mine = [g * PER_GROUP + n for n in range(PER_GROUP)]
        scores = []
        for i in mine:
            kw = jnp.concatenate([ak[:, hcols(i)], bk[:, hcols(i)], sk[:, hcols(i)]], axis=0)
            scores.append(lax.dot_general(sq[:, hcols(i)], kw, NT, preferred_element_type=F32))
        weights, sums = [], []
        none = jnp.zeros((BLK, BLK), BF16)
        for whole_s in scores:
            parts, inverse = [], []
            for b in range(2):
                s = whole_s[b * BLK:(b + 1) * BLK, b * BLK:(b + REACH + 1) * BLK] * scale
                s = jnp.concatenate([s[:, :REACH * BLK] + bias[b:b + 1, :],
                                     jnp.where(causal, s[:, REACH * BLK:], OFF)], axis=1)
                p = jnp.exp2(s - jnp.max(s, axis=1, keepdims=True))
                inverse.append(1.0 / jnp.sum(p, axis=1, keepdims=True))
                p = p.astype(BF16)
                parts.append(jnp.concatenate([p, none] if b == 0 else [none, p], axis=1))
            weights.append(jnp.concatenate(parts, axis=0))
            sums.append(jnp.concatenate(inverse, axis=0))
        for i, w, inverse in zip(mine, weights, sums):
            vw = jnp.concatenate([av[:, hcols(i)], bv[:, hcols(i)], sv[:, hcols(i)]], axis=0)
            sstage[:, hcols(i)] = (dot(w, vw) * inverse).astype(BF16)
        for copy in copies_out(1, sstage, out_soft, g):
            copy.start()
        copy_local(1, sstage, out_soft, g).start()

    def linear(g):
        causal = c_iota <= r_iota
        mine = [g * PER_GROUP + n for n in range(PER_GROUP)]
        none = jnp.zeros((BLK, BLK), BF16)
        scores = [lax.dot_general(lq[:, hcols(i)], lk[:, hcols(i)], NT, preferred_element_type=F32) for i in mine]
        left = []
        for i, s in zip(mine, scores):
            along, down = columns_of(i)
            top = s[:BLK, :BLK] * jnp.where(causal, jnp.exp(down[0] - along[0]), 0.0)
            across = s[BLK:, :BLK] * jnp.exp(down[1] - along[0])
            low = s[BLK:, BLK:] * jnp.where(causal, jnp.exp(down[1] - along[1]), 0.0)
            decayed = (lq[:, hcols(i)].astype(F32) * jnp.exp(jnp.concatenate(down, axis=0))).astype(BF16)
            left.append(jnp.concatenate([
                jnp.concatenate([top.astype(BF16), none], axis=1),
                jnp.concatenate([across.astype(BF16), low.astype(BF16)], axis=1)], axis=0))
            left[-1] = jnp.concatenate([left[-1], decayed], axis=1)
        for i, p in zip(mine, left):
            raw = dot(p, jnp.concatenate([lv[:, hcols(i)], inc[i]], axis=0))
            square = jnp.mean(raw * raw, axis=1, keepdims=True)
            lstage[:, hcols(i)] = (raw * lax.rsqrt(square + EPS) * gain[:, hcols(i)]).astype(BF16)
        for copy in copies_out(0, lstage, out_lin, g):
            copy.start()
        copy_local(0, lstage, out_lin, g).start()

    forward(0)

    stage = (c - odd) // 2

    def main(g, carry):
        @pl.when(g + AHEAD < groups)
        def _():
            start_kv(g + AHEAD)

        @pl.when(g + 1 < groups)
        def _():
            forward(g + 1)

        ready = RATE * (g - stage)
        for n in range(RATE):
            @pl.when(jnp.logical_and(ready + n >= 0, ready + n < groups))
            def _():
                chain(ready + n)

        @pl.when(g < groups)
        def _():
            softmax(g)

        for n in range(RATE):
            @pl.when(jnp.logical_and(ready + n >= 0, ready + n < groups))
            def _():
                linear(ready + n)
        return carry

    steps = max(groups, -(-groups // RATE) + (sections + 1) // 2 - 1)
    lax.fori_loop(0, steps, main, 0)

    def finish(g, carry):
        @pl.when(has_after)
        def _():
            for copy in copies_a(g):
                copy.wait_send()
            copy_x(g).wait_send()

        @pl.when(sends_b)
        def _():
            for copy in copies_b(g, (sk_hbm, sv_hbm)):
                copy.wait_send()
        copy_f(g).wait_send()
        for n, (stage, out) in enumerate(((lstage, out_lin), (sstage, out_soft))):
            copy_local(n, stage, out, g).wait()
            for copy in copies_out(n, stage, out, g):
                copy.wait()
        return carry

    lax.fori_loop(0, groups, finish, 0)


def local(sections, peers, linear_query, linear_key, linear_value, log_decay, norm_gain,
          soft_query, soft_key, soft_value, block_index, block_count):
    heads, length = log_decay.shape
    width = linear_query.shape[1]
    groups = heads // PER_GROUP
    carried = BF16 if sections <= 8 else F32
    smem, hbm = pl.BlockSpec(memory_space=pltpu.SMEM), pl.BlockSpec(memory_space=pl.ANY)
    rows = length // peers
    state = (heads, HD, HD)
    dma = pltpu.SemaphoreType.DMA
    return pl.pallas_call(
        functools.partial(kernel, sections, peers, heads),
        out_shape=[jax.ShapeDtypeStruct((rows, width * peers), BF16)] * 2,
        in_specs=[hbm] * 8 + [smem] * 2,
        out_specs=[hbm] * 2,
        scratch_shapes=[pltpu.VMEM((length, width), BF16)] * 12 + [
            pltpu.VMEM((heads, length), F32),
            pltpu.VMEM((1, width), F32),
            pltpu.VMEM((length // BLK, REACH * BLK), F32),
            pltpu.VMEM((heads, 1, length), F32),
            pltpu.VMEM((heads, 1, HD), F32),
            pltpu.VMEM((heads, 8, HD), F32),
            pltpu.VMEM((heads, 8, HD), F32),
            pltpu.VMEM(state, F32),
            pltpu.VMEM(state, BF16),
            pltpu.VMEM(state, BF16),
            pltpu.VMEM(state, carried),
            pltpu.VMEM(state, carried),
            pltpu.VMEM(state, BF16),
            dma((8,)), dma((2, groups)), dma((2, groups)), dma((2, groups)), dma((2, groups)),
            dma, dma, dma((groups,)), dma((groups,)), dma((groups,)), dma((groups,)),
            dma((2, groups, peers - 1)), dma((2, groups, peers - 1)), dma((2, groups)),
        ],
        compiler_params=pltpu.CompilerParams(
            collective_id=0, has_side_effects=True, vmem_limit_bytes=60 * 1024 * 1024),
        cost_estimate=pl.CostEstimate(flops=2_400_000_000, bytes_accessed=10_000_000, transcendentals=4_000_000),
    )(linear_query, linear_key, linear_value, log_decay, norm_gain.reshape(1, width),
      soft_query, soft_key, soft_value, block_index, block_count)


def solution(mesh):
    in_specs = (
        P("ctx", "head"), P("ctx", "head"), P("ctx", "head"), P("head", "ctx"), P("head"),
        P("ctx", "head"), P("ctx", "head"), P("ctx", "head"), P("ctx", None), P("ctx"),
    )
    out_specs = (P(("ctx", "head"), None), P(("ctx", "head"), None))
    body = functools.partial(local, mesh.shape["ctx"], mesh.shape["head"])
    return jax.shard_map(body, mesh=mesh, in_specs=in_specs, out_specs=out_specs, check_vma=False)
```

```python
import functools
import math

import jax
import jax.numpy as jnp
from jax import lax
from jax.experimental import pallas as pl
from jax.experimental.pallas import tpu as pltpu
from jax.sharding import PartitionSpec as P

BLK = 128
HD = 128
REACH = 4
PER_GROUP = 1
AHEAD = 4
RATE = 2
EPS = 1e-06
OFF = -1e30
F32 = jnp.float32
BF16 = jnp.bfloat16
MESH = pl.DeviceIdType.MESH
NT = (((1,), (1,)), ((), ()))
TN = (((0,), (0,)), ((), ()))


def dot(a, b):
    return jnp.dot(a, b, preferred_element_type=F32)


def kernel(sections, peers, heads,
           lq_hbm, lk_hbm, lv_hbm, ld_hbm, gain_hbm, sq_hbm, sk_hbm, sv_hbm, index, count,
           out_lin, out_soft,
           lq, lk, lv, sq, sk, sv, ak, av, bk, bv, lstage, sstage, ld, gain, bias,
           cc, last, exd, exp_, fown, fsend, frecv, xsend, xrecv, inc, load,
           a_send, a_recv, b_send, b_recv, d_send, d_recv, f_send, f_recv, x_send, x_recv, o_send, o_recv, o_local):
    groups = heads // PER_GROUP
    wide = PER_GROUP * HD
    length = lq_hbm.shape[0]
    rows = length // peers
    c, h = lax.axis_index("ctx"), lax.axis_index("head")
    odd = lax.rem(c, 2)
    even = 1 - odd
    partner = c + 1 - 2 * odd
    after, before = lax.rem(c + 2, sections), lax.rem(c + sections - 2, sections)
    has_after, has_before = c + 2 < sections, c >= 2
    has_b = c >= 1

    def cols(g):
        return pl.ds(pl.multiple_of(g * wide, wide), wide)

    def hcols(i):
        return pl.ds(pl.multiple_of(i * HD, HD), HD)

    def remote(src, dst, send, recv, where):
        return pltpu.make_async_remote_copy(
            src_ref=src, dst_ref=dst, send_sem=send, recv_sem=recv, device_id=where, device_id_type=MESH)

    def copies_a(g):
        return [remote(src.at[:, cols(g)], dst.at[:, cols(g)], a_send.at[n, g], a_recv.at[n, g], {"ctx": after})
                for n, (src, dst) in enumerate(((sk_hbm, ak), (sv_hbm, av)))]

    def copies_b(g, sources):
        return [remote(src.at[:, cols(g)], dst.at[:, cols(g)], b_send.at[n, g], b_recv.at[n, g], {"ctx": partner})
                for n, (src, dst) in enumerate(zip(sources, (bk, bv)))]

    def hd(g):
        return pl.ds(g * PER_GROUP, PER_GROUP)

    def copy_f(g):
        return remote(fsend.at[hd(g)], frecv.at[hd(g)], f_send.at[g], f_recv.at[g], {"ctx": partner})

    def copy_x(g):
        return remote(xsend.at[hd(g)], xrecv.at[hd(g)], x_send.at[g], x_recv.at[g], {"ctx": after})

    copy_d = remote(exd, exp_, d_send, d_recv, {"ctx": partner})

    def out_cols(g):
        return pl.ds(pl.multiple_of(h * (heads * HD) + g * wide, wide), wide)

    def copies_out(n, stage, out, g):
        made = []
        for k in range(1, peers):
            to = lax.rem(h + k, peers)
            made.append(remote(stage.at[pl.ds(pl.multiple_of(to * rows, rows), rows), cols(g)],
                               out.at[:, out_cols(g)],
                               o_send.at[n, g, k - 1], o_recv.at[n, g, k - 1], {"head": to}))
        return made

    def copy_local(n, stage, out, g):
        return pltpu.make_async_copy(stage.at[pl.ds(pl.multiple_of(h * rows, rows), rows), cols(g)],
                                     out.at[:, out_cols(g)], o_local.at[n, g])

    loads = [pltpu.make_async_copy(src, dst, load.at[n]) for n, (src, dst) in enumerate(
        ((lk_hbm, lk), (lv_hbm, lv), (lq_hbm, lq), (sq_hbm, sq), (sk_hbm, sk), (sv_hbm, sv),
         (ld_hbm, ld), (gain_hbm, gain)))]
    for n in (6, 7, 0, 1, 2, 3, 4, 5):
        loads[n].start()

    barrier = pltpu.get_barrier_semaphore()
    pl.semaphore_signal(barrier, inc=1, device_id={"ctx": partner}, device_id_type=MESH)
    for k in range(1, peers):
        pl.semaphore_signal(barrier, inc=1, device_id={"head": lax.rem(h + k, peers)}, device_id_type=MESH)

    @pl.when(has_after)
    def _():
        pl.semaphore_signal(barrier, inc=1, device_id={"ctx": after}, device_id_type=MESH)

    @pl.when(has_before)
    def _():
        pl.semaphore_signal(barrier, inc=1, device_id={"ctx": before}, device_id_type=MESH)

    pl.semaphore_wait(barrier, peers + has_after.astype(jnp.int32) + has_before.astype(jnp.int32))

    def start_kv(g):
        @pl.when(has_after)
        def _():
            for copy in copies_a(g):
                copy.start()

        @pl.when(odd == 0)
        def _():
            for copy in copies_b(g, (sk_hbm, sv_hbm)):
                copy.start()

    def sent_kv(g):
        @pl.when(has_after)
        def _():
            for copy in copies_a(g):
                copy.wait_send()

        @pl.when(odd == 0)
        def _():
            for copy in copies_b(g, (sk_hbm, sv_hbm)):
                copy.wait_send()

    start_kv(0)
    for n in (6, 7):
        loads[n].wait()
    lane = lax.broadcasted_iota(jnp.int32, (heads, length), 1)
    total = ld[...]
    shift = 1
    while shift < length:
        total = total + jnp.where(lane >= shift, pltpu.roll(total, shift, 1), 0.0)
        shift *= 2
    ends = jnp.broadcast_to(total[:, length - 1:], (heads, HD))
    whole = jnp.exp(ends)
    for i in range(heads):
        cc[i] = total[i:i + 1]
        last[i] = ends[i:i + 1]
        exd[i] = jnp.broadcast_to(whole[i:i + 1], (8, HD))
    copy_d.start()

    def columns_of(i):
        along = [jnp.broadcast_to(cc[i, :, pl.ds(b * BLK, BLK)], (BLK, BLK)) for b in range(2)]
        return along, [part.T for part in along]

    for n in (0, 1):
        loads[n].wait()

    def states(g, carry):
        for n in range(PER_GROUP):
            i = g * PER_GROUP + n
            down = jnp.concatenate(columns_of(i)[1], axis=0)
            kc = (lk[:, hcols(i)].astype(F32) * jnp.exp(last[i] - down)).astype(BF16)
            final = lax.dot_general(kc, lv[:, hcols(i)], TN, preferred_element_type=F32)
            fown[i] = final
            fsend[i] = final.astype(BF16)
        copy_f(g).start()

        @pl.when(g + 1 < AHEAD)
        def _():
            start_kv(g + 1)
        return carry

    lax.fori_loop(0, groups, states, 0)

    @pl.when(c < 2)
    def _():
        ak[...] = jnp.zeros_like(ak)
        av[...] = jnp.zeros_like(av)
        xrecv[...] = jnp.zeros_like(xrecv)

    @pl.when(c < 1)
    def _():
        bk[...] = jnp.zeros_like(bk)
        bv[...] = jnp.zeros_like(bv)

    copy_d.wait()
    here = length // BLK
    for b in range(here):
        tiles = []
        for w in range(REACH):
            block = here * c + b - REACH + w
            seen = [jnp.logical_and(slot < count[b], index[b, slot] == block) for slot in range(index.shape[1])]
            tiles.append(jnp.full((1, BLK), jnp.where(functools.reduce(jnp.logical_or, seen), 0.0, OFF), F32))
        bias[b:b + 1, :] = jnp.concatenate(tiles, axis=1)
    for n in range(2, 6):
        loads[n].wait()
    r_iota = lax.broadcasted_iota(jnp.int32, (BLK, BLK), 0)
    c_iota = lax.broadcasted_iota(jnp.int32, (BLK, BLK), 1)
    scale = math.log2(math.e) / math.sqrt(HD)

    def forward(g):
        @pl.when(has_before)
        def _():
            for copy in copies_a(g):
                copy.wait_recv()

        @pl.when(jnp.logical_and(odd == 1, has_before))
        def _():
            for copy in copies_b(g, (ak, av)):
                copy.start()

    def chain(g):
        copy_f(g).wait_recv()

        @pl.when(has_before)
        def _():
            copy_x(g).wait_recv()

        for n in range(PER_GROUP):
            i = g * PER_GROUP + n
            mine, other, x = fown[i], frecv[i].astype(F32), xrecv[i].astype(F32)
            d_mine, d_other = exd[i][:1], exp_[i][:1]
            is_odd = odd == 1
            mid = jnp.where(is_odd, d_other, d_mine) * x + jnp.where(is_odd, other, mine)
            xsend[i] = (jnp.where(is_odd, d_mine, d_other) * mid + jnp.where(is_odd, mine, other)).astype(xsend.dtype)
            inc[i] = jnp.where(is_odd, mid, x).astype(BF16)

        @pl.when(has_after)
        def _():
            copy_x(g).start()

    def softmax(g):
        @pl.when(has_b)
        def _():
            for copy in copies_b(g, (sk_hbm, sv_hbm)):
                copy.wait_recv()

        causal = c_iota <= r_iota
        mine = [g * PER_GROUP + n for n in range(PER_GROUP)]
        scores = []
        for i in mine:
            kw = jnp.concatenate([ak[:, hcols(i)], bk[:, hcols(i)], sk[:, hcols(i)]], axis=0)
            scores.append(lax.dot_general(sq[:, hcols(i)], kw, NT, preferred_element_type=F32))
        weights, sums = [], []
        none = jnp.zeros((BLK, BLK), BF16)
        for whole_s in scores:
            parts, inverse = [], []
            for b in range(2):
                s = whole_s[b * BLK:(b + 1) * BLK, b * BLK:(b + REACH + 1) * BLK] * scale
                s = jnp.concatenate([s[:, :REACH * BLK] + bias[b:b + 1, :],
                                     jnp.where(causal, s[:, REACH * BLK:], OFF)], axis=1)
                p = jnp.exp2(s - jnp.max(s, axis=1, keepdims=True))
                inverse.append(1.0 / jnp.sum(p, axis=1, keepdims=True))
                p = p.astype(BF16)
                parts.append(jnp.concatenate([p, none] if b == 0 else [none, p], axis=1))
            weights.append(jnp.concatenate(parts, axis=0))
            sums.append(jnp.concatenate(inverse, axis=0))
        for i, w, inverse in zip(mine, weights, sums):
            vw = jnp.concatenate([av[:, hcols(i)], bv[:, hcols(i)], sv[:, hcols(i)]], axis=0)
            sstage[:, hcols(i)] = (dot(w, vw) * inverse).astype(BF16)
        for copy in copies_out(1, sstage, out_soft, g):
            copy.start()
        copy_local(1, sstage, out_soft, g).start()

    def linear(g):
        causal = c_iota <= r_iota
        mine = [g * PER_GROUP + n for n in range(PER_GROUP)]
        none = jnp.zeros((BLK, BLK), BF16)
        scores = [lax.dot_general(lq[:, hcols(i)], lk[:, hcols(i)], NT, preferred_element_type=F32) for i in mine]
        left = []
        for i, s in zip(mine, scores):
            along, down = columns_of(i)
            top = s[:BLK, :BLK] * jnp.where(causal, jnp.exp(down[0] - along[0]), 0.0)
            across = s[BLK:, :BLK] * jnp.exp(down[1] - along[0])
            low = s[BLK:, BLK:] * jnp.where(causal, jnp.exp(down[1] - along[1]), 0.0)
            decayed = (lq[:, hcols(i)].astype(F32) * jnp.exp(jnp.concatenate(down, axis=0))).astype(BF16)
            left.append(jnp.concatenate([
                jnp.concatenate([top.astype(BF16), none], axis=1),
                jnp.concatenate([across.astype(BF16), low.astype(BF16)], axis=1)], axis=0))
            left[-1] = jnp.concatenate([left[-1], decayed], axis=1)
        for i, p in zip(mine, left):
            raw = dot(p, jnp.concatenate([lv[:, hcols(i)], inc[i]], axis=0))
            square = jnp.mean(raw * raw, axis=1, keepdims=True)
            lstage[:, hcols(i)] = (raw * lax.rsqrt(square + EPS) * gain[:, hcols(i)]).astype(BF16)
        for copy in copies_out(0, lstage, out_lin, g):
            copy.start()
        copy_local(0, lstage, out_lin, g).start()

    forward(0)

    stage = (c - odd) // 2

    def main(g, carry):
        @pl.when(g + AHEAD < groups)
        def _():
            sent_kv(g)
            start_kv(g + AHEAD)

        @pl.when(g + 1 < groups)
        def _():
            forward(g + 1)

        ready = RATE * (g - stage)
        for n in range(RATE):
            @pl.when(jnp.logical_and(ready + n >= 0, ready + n < groups))
            def _():
                chain(ready + n)

        @pl.when(g < groups)
        def _():
            softmax(g)

        for n in range(RATE):
            @pl.when(jnp.logical_and(ready + n >= 0, ready + n < groups))
            def _():
                linear(ready + n)
        return carry

    steps = max(groups, -(-groups // RATE) + (sections + 1) // 2 - 1)
    lax.fori_loop(0, steps, main, 0)

    def finish(g, carry):
        @pl.when(g >= groups - AHEAD)
        def _():
            sent_kv(g)

        @pl.when(has_after)
        def _():
            copy_x(g).wait_send()

        @pl.when(jnp.logical_and(odd == 1, has_before))
        def _():
            for copy in copies_b(g, (ak, av)):
                copy.wait_send()
        copy_f(g).wait_send()
        for n, (stage, out) in enumerate(((lstage, out_lin), (sstage, out_soft))):
            copy_local(n, stage, out, g).wait()
            for copy in copies_out(n, stage, out, g):
                copy.wait()
        return carry

    lax.fori_loop(0, groups, finish, 0)


def local(sections, peers, linear_query, linear_key, linear_value, log_decay, norm_gain,
          soft_query, soft_key, soft_value, block_index, block_count):
    heads, length = log_decay.shape
    width = linear_query.shape[1]
    groups = heads // PER_GROUP
    carried = BF16 if sections <= 8 else F32
    smem, hbm = pl.BlockSpec(memory_space=pltpu.SMEM), pl.BlockSpec(memory_space=pl.ANY)
    rows = length // peers
    state = (heads, HD, HD)
    dma = pltpu.SemaphoreType.DMA
    return pl.pallas_call(
        functools.partial(kernel, sections, peers, heads),
        out_shape=[jax.ShapeDtypeStruct((rows, width * peers), BF16)] * 2,
        in_specs=[hbm] * 8 + [smem] * 2,
        out_specs=[hbm] * 2,
        scratch_shapes=[pltpu.VMEM((length, width), BF16)] * 12 + [
            pltpu.VMEM((heads, length), F32),
            pltpu.VMEM((1, width), F32),
            pltpu.VMEM((length // BLK, REACH * BLK), F32),
            pltpu.VMEM((heads, 1, length), F32),
            pltpu.VMEM((heads, 1, HD), F32),
            pltpu.VMEM((heads, 8, HD), F32),
            pltpu.VMEM((heads, 8, HD), F32),
            pltpu.VMEM(state, F32),
            pltpu.VMEM(state, BF16),
            pltpu.VMEM(state, BF16),
            pltpu.VMEM(state, carried),
            pltpu.VMEM(state, carried),
            pltpu.VMEM(state, BF16),
            dma((8,)), dma((2, groups)), dma((2, groups)), dma((2, groups)), dma((2, groups)),
            dma, dma, dma((groups,)), dma((groups,)), dma((groups,)), dma((groups,)),
            dma((2, groups, peers - 1)), dma((2, groups, peers - 1)), dma((2, groups)),
        ],
        compiler_params=pltpu.CompilerParams(
            collective_id=0, has_side_effects=True, vmem_limit_bytes=60 * 1024 * 1024),
        cost_estimate=pl.CostEstimate(flops=2_400_000_000, bytes_accessed=10_000_000, transcendentals=4_000_000),
    )(linear_query, linear_key, linear_value, log_decay, norm_gain.reshape(1, width),
      soft_query, soft_key, soft_value, block_index, block_count)


def solution(mesh):
    in_specs = (
        P("ctx", "head"), P("ctx", "head"), P("ctx", "head"), P("head", "ctx"), P("head"),
        P("ctx", "head"), P("ctx", "head"), P("ctx", "head"), P("ctx", None), P("ctx"),
    )
    out_specs = (P(("ctx", "head"), None), P(("ctx", "head"), None))
    body = functools.partial(local, mesh.shape["ctx"], mesh.shape["head"])
    return jax.shard_map(body, mesh=mesh, in_specs=in_specs, out_specs=out_specs, check_vma=False)
```

```python
import functools
import math

import jax
import jax.numpy as jnp
from jax import lax
from jax.experimental import pallas as pl
from jax.experimental.pallas import tpu as pltpu
from jax.sharding import PartitionSpec as P

BLK = 128
HD = 128
REACH = 4
PER_GROUP = 1
AHEAD = 4
RATE = 2
EPS = 1e-06
OFF = -1e30
F32 = jnp.float32
BF16 = jnp.bfloat16
MESH = pl.DeviceIdType.MESH
NT = (((1,), (1,)), ((), ()))
TN = (((0,), (0,)), ((), ()))


def dot(a, b):
    return jnp.dot(a, b, preferred_element_type=F32)


def kernel(sections, peers, heads,
           lq_hbm, lk_hbm, lv_hbm, ld_hbm, gain_hbm, sq_hbm, sk_hbm, sv_hbm, index, count,
           out_lin, out_soft,
           lq, lk, lv, sq, sk, sv, ak, av, bk, bv, lstage, sstage, ld, gain, bias,
           cc, last, exd, exp_, fown, fsend, frecv, xsend, xrecv, inc, load, kv_load,
           a_send, a_recv, b_send, b_recv, d_send, d_recv, f_send, f_recv, x_send, x_recv, o_send, o_recv, o_local):
    groups = heads // PER_GROUP
    wide = PER_GROUP * HD
    length = lq_hbm.shape[0]
    rows = length // peers
    c, h = lax.axis_index("ctx"), lax.axis_index("head")
    odd = lax.rem(c, 2)
    even = 1 - odd
    partner = c + 1 - 2 * odd
    after, before = lax.rem(c + 2, sections), lax.rem(c + sections - 2, sections)
    has_after, has_before = c + 2 < sections, c >= 2
    has_b = c >= 1

    def cols(g):
        return pl.ds(pl.multiple_of(g * wide, wide), wide)

    def hcols(i):
        return pl.ds(pl.multiple_of(i * HD, HD), HD)

    def remote(src, dst, send, recv, where):
        return pltpu.make_async_remote_copy(
            src_ref=src, dst_ref=dst, send_sem=send, recv_sem=recv, device_id=where, device_id_type=MESH)

    def copies_a(g):
        return [remote(src.at[hd(g)], dst.at[hd(g)], a_send.at[n, g], a_recv.at[n, g], {"ctx": after})
                for n, (src, dst) in enumerate(((sk, ak), (sv, av)))]

    def copies_b(g, sources):
        return [remote(src.at[hd(g)], dst.at[hd(g)], b_send.at[n, g], b_recv.at[n, g], {"ctx": partner})
                for n, (src, dst) in enumerate(zip(sources, (bk, bv)))]

    def hd(g):
        return pl.ds(g * PER_GROUP, PER_GROUP)

    def copy_f(g):
        return remote(fsend.at[hd(g)], frecv.at[hd(g)], f_send.at[g], f_recv.at[g], {"ctx": partner})

    def copy_x(g):
        return remote(xsend.at[hd(g)], xrecv.at[hd(g)], x_send.at[g], x_recv.at[g], {"ctx": after})

    copy_d = remote(exd, exp_, d_send, d_recv, {"ctx": partner})

    def out_cols(g):
        return pl.ds(pl.multiple_of(h * (heads * HD) + g * wide, wide), wide)

    def copies_out(n, stage, out, g):
        made = []
        for k in range(1, peers):
            to = lax.rem(h + k, peers)
            made.append(remote(stage.at[pl.ds(pl.multiple_of(to * rows, rows), rows), cols(g)],
                               out.at[:, out_cols(g)],
                               o_send.at[n, g, k - 1], o_recv.at[n, g, k - 1], {"head": to}))
        return made

    def copy_local(n, stage, out, g):
        return pltpu.make_async_copy(stage.at[pl.ds(pl.multiple_of(h * rows, rows), rows), cols(g)],
                                     out.at[:, out_cols(g)], o_local.at[n, g])

    loads = [pltpu.make_async_copy(src, dst, load.at[n]) for n, (src, dst) in enumerate(
        ((lk_hbm, lk), (lv_hbm, lv), (lq_hbm, lq), (sq_hbm, sq),
         (ld_hbm, ld), (gain_hbm, gain)))]

    def kv_loads(i):
        return [pltpu.make_async_copy(src.at[:, hcols(i)], dst.at[i], kv_load.at[n, i])
                for n, (src, dst) in enumerate(((sk_hbm, sk), (sv_hbm, sv)))]

    def load_kv(i, carry):
        for copy in kv_loads(i):
            copy.start()
        return carry

    lax.fori_loop(0, AHEAD * PER_GROUP, load_kv, 0)
    for n in (4, 5, 0, 1, 2, 3):
        loads[n].start()
    lax.fori_loop(AHEAD * PER_GROUP, heads, load_kv, 0)

    barrier = pltpu.get_barrier_semaphore()
    pl.semaphore_signal(barrier, inc=1, device_id={"ctx": partner}, device_id_type=MESH)
    for k in range(1, peers):
        pl.semaphore_signal(barrier, inc=1, device_id={"head": lax.rem(h + k, peers)}, device_id_type=MESH)

    @pl.when(has_after)
    def _():
        pl.semaphore_signal(barrier, inc=1, device_id={"ctx": after}, device_id_type=MESH)

    @pl.when(has_before)
    def _():
        pl.semaphore_signal(barrier, inc=1, device_id={"ctx": before}, device_id_type=MESH)

    pl.semaphore_wait(barrier, peers + has_after.astype(jnp.int32) + has_before.astype(jnp.int32))

    def start_kv(g):
        for n in range(PER_GROUP):
            for copy in kv_loads(g * PER_GROUP + n):
                copy.wait()

        @pl.when(has_after)
        def _():
            for copy in copies_a(g):
                copy.start()

        @pl.when(odd == 0)
        def _():
            for copy in copies_b(g, (sk, sv)):
                copy.start()

    def sent_kv(g):
        @pl.when(has_after)
        def _():
            for copy in copies_a(g):
                copy.wait_send()

        @pl.when(odd == 0)
        def _():
            for copy in copies_b(g, (sk, sv)):
                copy.wait_send()

    start_kv(0)
    for n in (4, 5):
        loads[n].wait()
    lane = lax.broadcasted_iota(jnp.int32, (heads, length), 1)
    total = ld[...]
    shift = 1
    while shift < length:
        total = total + jnp.where(lane >= shift, pltpu.roll(total, shift, 1), 0.0)
        shift *= 2
    ends = jnp.broadcast_to(total[:, length - 1:], (heads, HD))
    whole = jnp.exp(ends)
    for i in range(heads):
        cc[i] = total[i:i + 1]
        last[i] = ends[i:i + 1]
        exd[i] = jnp.broadcast_to(whole[i:i + 1], (8, HD))
    copy_d.start()

    def columns_of(i):
        along = [jnp.broadcast_to(cc[i, :, pl.ds(b * BLK, BLK)], (BLK, BLK)) for b in range(2)]
        return along, [part.T for part in along]

    for n in (0, 1):
        loads[n].wait()

    def states(g, carry):
        for n in range(PER_GROUP):
            i = g * PER_GROUP + n
            down = jnp.concatenate(columns_of(i)[1], axis=0)
            kc = (lk[:, hcols(i)].astype(F32) * jnp.exp(last[i] - down)).astype(BF16)
            final = lax.dot_general(kc, lv[:, hcols(i)], TN, preferred_element_type=F32)
            fown[i] = final
            fsend[i] = final.astype(BF16)
        copy_f(g).start()

        @pl.when(g + 1 < AHEAD)
        def _():
            start_kv(g + 1)
        return carry

    lax.fori_loop(0, groups, states, 0)

    @pl.when(c < 2)
    def _():
        ak[...] = jnp.zeros_like(ak)
        av[...] = jnp.zeros_like(av)
        xrecv[...] = jnp.zeros_like(xrecv)

    @pl.when(c < 1)
    def _():
        bk[...] = jnp.zeros_like(bk)
        bv[...] = jnp.zeros_like(bv)

    copy_d.wait()
    here = length // BLK
    for b in range(here):
        tiles = []
        for w in range(REACH):
            block = here * c + b - REACH + w
            seen = [jnp.logical_and(slot < count[b], index[b, slot] == block) for slot in range(index.shape[1])]
            tiles.append(jnp.full((1, BLK), jnp.where(functools.reduce(jnp.logical_or, seen), 0.0, OFF), F32))
        bias[b:b + 1, :] = jnp.concatenate(tiles, axis=1)
    for n in (2, 3):
        loads[n].wait()
    r_iota = lax.broadcasted_iota(jnp.int32, (BLK, BLK), 0)
    c_iota = lax.broadcasted_iota(jnp.int32, (BLK, BLK), 1)
    scale = math.log2(math.e) / math.sqrt(HD)

    def forward(g):
        @pl.when(has_before)
        def _():
            for copy in copies_a(g):
                copy.wait_recv()

        @pl.when(jnp.logical_and(odd == 1, has_before))
        def _():
            for copy in copies_b(g, (ak, av)):
                copy.start()

    def chain(g):
        copy_f(g).wait_recv()

        @pl.when(has_before)
        def _():
            copy_x(g).wait_recv()

        for n in range(PER_GROUP):
            i = g * PER_GROUP + n
            mine, other, x = fown[i], frecv[i].astype(F32), xrecv[i].astype(F32)
            d_mine, d_other = exd[i][:1], exp_[i][:1]
            is_odd = odd == 1
            mid = jnp.where(is_odd, d_other, d_mine) * x + jnp.where(is_odd, other, mine)
            xsend[i] = (jnp.where(is_odd, d_mine, d_other) * mid + jnp.where(is_odd, mine, other)).astype(xsend.dtype)
            inc[i] = jnp.where(is_odd, mid, x).astype(BF16)

        @pl.when(has_after)
        def _():
            copy_x(g).start()

    def softmax(g):
        @pl.when(has_b)
        def _():
            for copy in copies_b(g, (sk, sv)):
                copy.wait_recv()

        causal = c_iota <= r_iota
        mine = [g * PER_GROUP + n for n in range(PER_GROUP)]
        scores = []
        for i in mine:
            kw = jnp.concatenate([ak[i], bk[i], sk[i]], axis=0)
            scores.append(lax.dot_general(sq[:, hcols(i)], kw, NT, preferred_element_type=F32))
        weights, sums = [], []
        none = jnp.zeros((BLK, BLK), BF16)
        for whole_s in scores:
            parts, inverse = [], []
            for b in range(2):
                s = whole_s[b * BLK:(b + 1) * BLK, b * BLK:(b + REACH + 1) * BLK] * scale
                s = jnp.concatenate([s[:, :REACH * BLK] + bias[b:b + 1, :],
                                     jnp.where(causal, s[:, REACH * BLK:], OFF)], axis=1)
                p = jnp.exp2(s - jnp.max(s, axis=1, keepdims=True))
                inverse.append(1.0 / jnp.sum(p, axis=1, keepdims=True))
                p = p.astype(BF16)
                parts.append(jnp.concatenate([p, none] if b == 0 else [none, p], axis=1))
            weights.append(jnp.concatenate(parts, axis=0))
            sums.append(jnp.concatenate(inverse, axis=0))
        for i, w, inverse in zip(mine, weights, sums):
            vw = jnp.concatenate([av[i], bv[i], sv[i]], axis=0)
            sstage[:, hcols(i)] = (dot(w, vw) * inverse).astype(BF16)
        for copy in copies_out(1, sstage, out_soft, g):
            copy.start()
        copy_local(1, sstage, out_soft, g).start()

    def linear(g):
        causal = c_iota <= r_iota
        mine = [g * PER_GROUP + n for n in range(PER_GROUP)]
        none = jnp.zeros((BLK, BLK), BF16)
        scores = [lax.dot_general(lq[:, hcols(i)], lk[:, hcols(i)], NT, preferred_element_type=F32) for i in mine]
        left = []
        for i, s in zip(mine, scores):
            along, down = columns_of(i)
            top = s[:BLK, :BLK] * jnp.where(causal, jnp.exp(down[0] - along[0]), 0.0)
            across = s[BLK:, :BLK] * jnp.exp(down[1] - along[0])
            low = s[BLK:, BLK:] * jnp.where(causal, jnp.exp(down[1] - along[1]), 0.0)
            decayed = (lq[:, hcols(i)].astype(F32) * jnp.exp(jnp.concatenate(down, axis=0))).astype(BF16)
            left.append(jnp.concatenate([
                jnp.concatenate([top.astype(BF16), none], axis=1),
                jnp.concatenate([across.astype(BF16), low.astype(BF16)], axis=1)], axis=0))
            left[-1] = jnp.concatenate([left[-1], decayed], axis=1)
        for i, p in zip(mine, left):
            raw = dot(p, jnp.concatenate([lv[:, hcols(i)], inc[i]], axis=0))
            square = jnp.mean(raw * raw, axis=1, keepdims=True)
            lstage[:, hcols(i)] = (raw * lax.rsqrt(square + EPS) * gain[:, hcols(i)]).astype(BF16)
        for copy in copies_out(0, lstage, out_lin, g):
            copy.start()
        copy_local(0, lstage, out_lin, g).start()

    forward(0)

    stage = (c - odd) // 2

    def main(g, carry):
        @pl.when(g + AHEAD < groups)
        def _():
            sent_kv(g)
            start_kv(g + AHEAD)

        @pl.when(g + 1 < groups)
        def _():
            forward(g + 1)

        ready = RATE * (g - stage)
        for n in range(RATE):
            @pl.when(jnp.logical_and(ready + n >= 0, ready + n < groups))
            def _():
                chain(ready + n)

        @pl.when(g < groups)
        def _():
            softmax(g)

        for n in range(RATE):
            @pl.when(jnp.logical_and(ready + n >= 0, ready + n < groups))
            def _():
                linear(ready + n)
        return carry

    steps = max(groups, -(-groups // RATE) + (sections + 1) // 2 - 1)
    lax.fori_loop(0, steps, main, 0)

    def finish(g, carry):
        @pl.when(g >= groups - AHEAD)
        def _():
            sent_kv(g)

        @pl.when(has_after)
        def _():
            copy_x(g).wait_send()

        @pl.when(jnp.logical_and(odd == 1, has_before))
        def _():
            for copy in copies_b(g, (ak, av)):
                copy.wait_send()
        copy_f(g).wait_send()
        for n, (stage, out) in enumerate(((lstage, out_lin), (sstage, out_soft))):
            copy_local(n, stage, out, g).wait()
            for copy in copies_out(n, stage, out, g):
                copy.wait()
        return carry

    lax.fori_loop(0, groups, finish, 0)


def local(sections, peers, linear_query, linear_key, linear_value, log_decay, norm_gain,
          soft_query, soft_key, soft_value, block_index, block_count):
    heads, length = log_decay.shape
    width = linear_query.shape[1]
    groups = heads // PER_GROUP
    carried = BF16 if sections <= 8 else F32
    smem, hbm = pl.BlockSpec(memory_space=pltpu.SMEM), pl.BlockSpec(memory_space=pl.ANY)
    rows = length // peers
    state = (heads, HD, HD)
    dma = pltpu.SemaphoreType.DMA
    return pl.pallas_call(
        functools.partial(kernel, sections, peers, heads),
        out_shape=[jax.ShapeDtypeStruct((rows, width * peers), BF16)] * 2,
        in_specs=[hbm] * 8 + [smem] * 2,
        out_specs=[hbm] * 2,
        scratch_shapes=[pltpu.VMEM((length, width), BF16)] * 4 + [pltpu.VMEM((heads, length, HD), BF16)] * 6 + [
            pltpu.VMEM((length, width), BF16), pltpu.VMEM((length, width), BF16),
            pltpu.VMEM((heads, length), F32),
            pltpu.VMEM((1, width), F32),
            pltpu.VMEM((length // BLK, REACH * BLK), F32),
            pltpu.VMEM((heads, 1, length), F32),
            pltpu.VMEM((heads, 1, HD), F32),
            pltpu.VMEM((heads, 8, HD), F32),
            pltpu.VMEM((heads, 8, HD), F32),
            pltpu.VMEM(state, F32),
            pltpu.VMEM(state, BF16),
            pltpu.VMEM(state, BF16),
            pltpu.VMEM(state, carried),
            pltpu.VMEM(state, carried),
            pltpu.VMEM(state, BF16),
            dma((6,)), dma((2, heads)), dma((2, groups)), dma((2, groups)), dma((2, groups)), dma((2, groups)),
            dma, dma, dma((groups,)), dma((groups,)), dma((groups,)), dma((groups,)),
            dma((2, groups, peers - 1)), dma((2, groups, peers - 1)), dma((2, groups)),
        ],
        compiler_params=pltpu.CompilerParams(
            collective_id=0, has_side_effects=True, vmem_limit_bytes=60 * 1024 * 1024),
        cost_estimate=pl.CostEstimate(flops=2_400_000_000, bytes_accessed=10_000_000, transcendentals=4_000_000),
    )(linear_query, linear_key, linear_value, log_decay, norm_gain.reshape(1, width),
      soft_query, soft_key, soft_value, block_index, block_count)


def solution(mesh):
    in_specs = (
        P("ctx", "head"), P("ctx", "head"), P("ctx", "head"), P("head", "ctx"), P("head"),
        P("ctx", "head"), P("ctx", "head"), P("ctx", "head"), P("ctx", None), P("ctx"),
    )
    out_specs = (P(("ctx", "head"), None), P(("ctx", "head"), None))
    body = functools.partial(local, mesh.shape["ctx"], mesh.shape["head"])
    return jax.shard_map(body, mesh=mesh, in_specs=in_specs, out_specs=out_specs, check_vma=False)
```
